256 devices in a mesh: ctx: 128 (over x, y, z), head: 2 (over core).
Axes of the slice: x: 4, y: 4, z: 8, core: 2. Of those that a mesh axis runs over, the one named last changes fastest.
Arguments:
- queries: bfloat16 [65536, 2048], P('ctx', 'head'), may hold values from -1.5 to 1.5
- key_vectors: bfloat16 [65536, 2048], P('ctx', 'head'), may hold values from -1.5 to 1.5
- values: bfloat16 [65536, 2048], P('ctx', 'head'), may hold values from -4 to 4
- features: bfloat16 [16, 128, 256], P('head'), may hold values from -4 to 4
- norm_gain: bfloat16 [2048], P('head'), may hold values from 0.099609375 to 1.8984375
- out_weight: bfloat16 [2048, 2048], P('head'), may hold values from -0.125 to 0.125
Outputs:
- projected: bfloat16 [65536, 2048], P(('ctx', 'head'))
The draws below stay inside these ranges and needn't reach their ends.
All inputs are finite; a program needn't handle non-finite values.
Results may differ from the reference program's by a relative error of at most 0.0059.
Values may be sent and summed in bfloat16 or wider, within the bound.
A program may use at most 320 MiB of HBM per device.

```python
import jax
import jax.numpy as jnp
from jax import lax

D = 2048
H = 16
DH = 128
M = 256
BLK = 256
TOKENS = 65536


def steps_of(stream_key, dims, split, smallest, high):
    factor_of = 1.0
    for position, parts in split:
        draws = jax.random.uniform(jax.random.fold_in(jax.random.fold_in(stream_key, 6), position), (parts,), jnp.float32, smallest / len(split), high / len(split))
        factor_of = factor_of * jnp.repeat(jnp.exp(draws), dims[position] // parts).reshape((-1,) + (1,) * (len(dims) - 1 - position))
    return factor_of


def noise(rng, dims, deviation, reach, cuts=(), dtype=jnp.bfloat16):
    values = jax.random.normal(rng, dims, jnp.float32) * deviation
    if len(cuts) > 0:
        values = steps_of(rng, dims, cuts, -0.22, 0.18) * values
    return jnp.clip(values, min=-reach, max=reach).astype(dtype)


def setup_inputs(seed: int = 0) -> dict:
    streams_of = jax.random.split(jax.random.key(seed), 7)
    queries = noise(streams_of[0], (TOKENS, H * DH), 0.35, 1.5, ((0, 128), (1, 2)))
    key_vectors = noise(streams_of[1], (TOKENS, H * DH), 0.35, 1.5, ((0, 128), (1, 2)))
    values = noise(streams_of[2], (TOKENS, H * DH), 1.0, 4.0, ((0, 128), (1, 2)))
    features = noise(streams_of[3], (H, DH, M), 1.0, 4.0, ((0, 2),))
    norm_gain = jnp.clip(1.0 + 0.18 * jax.random.normal(streams_of[4], (H * DH,), jnp.float32), 0.099609375, 1.8984375).astype(jnp.bfloat16)
    out_weight = noise(streams_of[5], (H * DH, D), (H * DH) ** -0.5, 0.125, ((0, 2),))
    return {"queries": queries, "key_vectors": key_vectors, "values": values, "features": features, "norm_gain": norm_gain, "out_weight": out_weight}


epsilon = 1e-05

def positive(vectors, matrix):
    widened = vectors.astype(jnp.float32)
    feature_scale = DH ** (-0.25)
    linear_part = jnp.einsum('rhd,hdm->rhm', widened, matrix.astype(jnp.float32)) * feature_scale
    squares = lax.optimization_barrier(jnp.sum(widened * widened, axis=-1, keepdims=True)) * (feature_scale * feature_scale)
    return (jnp.exp(linear_part - 0.5 * squares) * M ** (-0.5)).astype(jnp.bfloat16)

def reference(queries, key_vectors, values, features, norm_gain, out_weight):
    blocks = TOKENS // BLK
    query_blocks = queries.reshape(blocks, BLK, H, DH)
    key_blocks = key_vectors.reshape(blocks, BLK, H, DH)
    value_blocks = values.reshape(blocks, BLK, H, DH)
    causal_mask = jnp.arange(BLK)[:, None] >= jnp.arange(BLK)[None, :]
    gain_heads = norm_gain.astype(jnp.float32).reshape(H, DH)

    def advance(cumulative_state, pieces):
        query_block, key_block, value_tile_rows = pieces
        query_feature_map = positive(query_block, features).astype(jnp.float32)
        key_feature_map = positive(key_block, features).astype(jnp.float32)
        value_augmented = value_tile_rows.astype(jnp.float32)
        scores = jnp.einsum('ihm,jhm->hij', query_feature_map, key_feature_map)
        weights = jnp.where(causal_mask[None], scores, jnp.float32(0.0)).astype(jnp.bfloat16)
        local_term = jnp.einsum('hij,jhd->ihd', weights.astype(jnp.float32), value_augmented)
        preceding_block_term = jnp.einsum('gnp,npf->gnf', query_feature_map, cumulative_state.astype(jnp.bfloat16).astype(jnp.float32))
        numerator = preceding_block_term + local_term
        normed = numerator * lax.rsqrt(lax.optimization_barrier(jnp.mean(numerator * numerator, axis=-1, keepdims=True)) + epsilon) * gain_heads
        attended = normed.reshape(BLK, H * DH).astype(jnp.bfloat16)
        block_kv_state = jnp.einsum('woa,wog->oag', key_feature_map, value_augmented)
        projected = jnp.dot(attended, out_weight, preferred_element_type=jnp.float32).astype(jnp.bfloat16)
        return (cumulative_state + block_kv_state, projected)
    initial = jnp.zeros((H, M, DH), jnp.float32)
    _, outputs = lax.scan(advance, initial, (query_blocks, key_blocks, value_blocks))
    return outputs.reshape(TOKENS, D)
```

```python
import jax
import jax.numpy as jnp
from jax import lax
from jax.experimental import pallas as pl
from jax.experimental.pallas import tpu as pltpu
from jax.sharding import PartitionSpec as P

MESH = pl.DeviceIdType.MESH
F32 = jnp.float32
BF16 = jnp.bfloat16
BLK = 256
NX, NY, NZ = 4, 4, 8
CHUNKS = 2
OUT_TILES = 4
EPSILON = 1e-05
ORDER = (4, 3, 5, 2, 6, 1, 7)


def dot(a, b, contract=((1,), (0,))):
    return lax.dot_general(a, b, (contract, ((), ())), preferred_element_type=F32)


def halves(squared):
    high = squared.astype(BF16)
    return high, (squared - high.astype(F32)).astype(BF16)


def kernel(
    q_hbm, k_hbm, v_hbm, f_hbm, gain_hbm, w_hbm, out_hbm,
    q_ref, k_ref, v_ref, f_ref, gain_ref, w_ref, out_ref,
    kft, qf, local, first, state_send, state_recv, y_send, y_recv, x_send, x_recv,
    prefix_send, prefix_recv, att, base,
    load_sem, out_sem, w_sems, s_ssem, s_rsem, y_ssem, y_rsem, x_ssem, x_rsem, p_ssem, p_rsem, a_ssem, a_rsem,
):
    heads, dh, m = f_ref.shape
    rows = q_ref.shape[0]
    width = heads * dh
    scale = dh ** (-0.25)
    log2e = 1.4426950408889634
    shift = 0.5 * (m.bit_length() - 1)
    part = m // CHUNKS
    me = lax.axis_index("ctx")
    core = lax.axis_index("head")
    z = lax.rem(me, NZ)
    y = lax.rem(me // NZ, NY)
    x = me // (NZ * NY)

    def at_z(d):
        return lax.rem(z + d, NZ)

    def z_device(d):
        return me - z + at_z(d)

    def y_device(d):
        return me + (lax.rem(y + d, NY) - y) * NZ

    def x_device(d):
        return me + (lax.rem(x + d, NX) - x) * (NZ * NY)

    def head_columns(h):
        return pl.ds(pl.multiple_of(h * dh, dh), dh)

    own_rows = pl.ds(pl.multiple_of(core * width, width), width)

    loads = [
        pltpu.make_async_copy(src, dst, load_sem.at[i])
        for i, (src, dst) in enumerate(
            (
                (f_hbm, f_ref),
                (k_hbm, k_ref),
                (v_hbm, v_ref),
                (q_hbm, q_ref),
                (gain_hbm, gain_ref),
                (w_hbm, w_ref.at[own_rows, :]),
            )
        )
    ]
    for load in loads:
        load.start()

    barrier = pltpu.get_barrier_semaphore()
    partners = (
        [{"ctx": z_device(d)} for d in range(1, NZ)]
        + [{"ctx": y_device(d)} for d in range(1, NY)]
        + [{"ctx": x_device(d)} for d in range(1, NX)]
        + [{"head": 1 - core}]
    )
    for partner in partners:
        pl.semaphore_signal(barrier, inc=1, device_id=partner, device_id_type=MESH)
    pl.semaphore_wait(barrier, len(partners))

    w_copy = pltpu.make_async_remote_copy(
        src_ref=w_hbm, dst_ref=w_ref.at[own_rows, :], send_sem=w_sems.at[0], recv_sem=w_sems.at[1],
        device_id={"head": 1 - core}, device_id_type=MESH,
    )
    w_copy.start()

    def state_copy(c, d):
        return pltpu.make_async_remote_copy(
            src_ref=state_send.at[c, at_z(d)], dst_ref=state_recv.at[c, z],
            send_sem=s_ssem.at[c, d], recv_sem=s_rsem.at[c, z],
            device_id={"ctx": z_device(d)}, device_id_type=MESH,
        )

    def prefix_copy(c, d):
        return pltpu.make_async_remote_copy(
            src_ref=prefix_send.at[c, at_z(d)], dst_ref=prefix_recv.at[c, z],
            send_sem=p_ssem.at[c, d], recv_sem=p_rsem.at[c, z],
            device_id={"ctx": z_device(d)}, device_id_type=MESH,
        )

    def y_copy(c, d):
        return pltpu.make_async_remote_copy(
            src_ref=y_send.at[c], dst_ref=y_recv.at[c, y], send_sem=y_ssem.at[c, d], recv_sem=y_rsem.at[c, y],
            device_id={"ctx": y_device(d)}, device_id_type=MESH,
        )

    def x_copy(c, d):
        return pltpu.make_async_remote_copy(
            src_ref=x_send.at[c], dst_ref=x_recv.at[c, x], send_sem=x_ssem.at[c, d], recv_sem=x_rsem.at[c, x],
            device_id={"ctx": x_device(d)}, device_id_type=MESH,
        )

    def arrival(ref, sem, device_id):
        return pltpu.make_async_remote_copy(
            src_ref=ref, dst_ref=ref, send_sem=sem, recv_sem=sem, device_id=device_id, device_id_type=MESH
        )

    loads[0].wait()
    loads[1].wait()
    loads[2].wait()
    ones_row = jnp.ones((8, dh), BF16)

    def key_head(h):
        cols = head_columns(h)
        k = k_ref[:, cols]
        v = v_ref[:, cols]
        linear = dot(f_ref[h].T, k, ((1,), (1,)))
        wide = k.astype(F32)
        high, low = halves(wide * wide)
        squares = (dot(ones_row, high, ((1,), (1,))) + dot(ones_row, low, ((1,), (1,))))[0:1]
        feats = jnp.exp2(
            linear * (scale * log2e) - (squares * (0.5 * scale * scale * log2e) + shift)
        ).astype(BF16)
        kft[h] = feats
        one = dot(feats[:, :BLK], v[:BLK])
        two = dot(feats[:, BLK:], v[BLK:])
        first[h] = one.astype(BF16)
        return (one + two).astype(BF16)

    def key_step(i, carry):
        d = lax.select(i % 2 == 0, NZ // 2 + i // 2, NZ // 2 - 1 - i // 2)
        d = lax.rem(d, NZ)
        h = at_z(d)
        state = key_head(h)
        for c in range(CHUNKS):
            state_send[c, h] = state[c * part : (c + 1) * part]
        state_copy(0, d).start()
        return carry

    lax.fori_loop(0, NZ - 1, key_step, 0)
    state = key_head(z)
    for c in range(CHUNKS):
        state_recv[c, z] = state[c * part : (c + 1) * part]
    for c in range(1, CHUNKS):
        for d in ORDER:
            state_copy(c, d).start()

    loads[3].wait()
    ones_square = jnp.ones((dh, dh), BF16)
    mask = lax.broadcasted_iota(jnp.int32, (BLK, BLK), 0) >= lax.broadcasted_iota(jnp.int32, (BLK, BLK), 1)

    def query_head(h, carry):
        cols = head_columns(h)
        q = q_ref[:, cols]
        wide = q.astype(F32)
        high, low = halves(wide * wide)
        squares = dot(high, ones_square) + dot(low, ones_square)
        away = squares * (0.5 * scale * scale * log2e) + shift
        linear = dot(q, f_ref[h])
        feats = jnp.exp2(
            linear * (scale * log2e) - jnp.concatenate([away] * (m // dh), axis=1)
        ).astype(BF16)
        qf[h] = feats
        for b in range(rows // BLK):
            span = slice(b * BLK, (b + 1) * BLK)
            scores = dot(feats[span], kft[h, :, span])
            weights = jnp.where(mask, scores, 0.0).astype(BF16)
            term = dot(weights, v_ref[span, cols])
            if b > 0:
                term = term + dot(feats[span], first[h])
            local[span, cols] = term
        return carry

    lax.fori_loop(0, heads, query_head, 0)

    for c in range(CHUNKS):
        for d in range(1, NZ):
            s = at_z(d)
            arrival(state_recv.at[c, s], s_rsem.at[c, s], {"ctx": z_device(d)}).wait_recv()
        total = jnp.zeros((part, dh), F32)
        for s in range(NZ):
            total = total + state_recv[c, s].astype(F32)
        line = total.astype(BF16)
        y_send[c] = line
        y_recv[c, y] = line
        for d in range(1, NY):
            y_copy(c, d).start()
        for d in range(1, NY):
            s = lax.rem(y + d, NY)
            arrival(y_recv.at[c, s], y_rsem.at[c, s], {"ctx": y_device(d)}).wait_recv()
        total = jnp.zeros((part, dh), F32)
        before = jnp.zeros((part, dh), F32)
        for s in range(NY):
            one = y_recv[c, s].astype(F32)
            total = total + one
            before = before + jnp.where(s < y, one, 0.0)
        base[...] = before
        plane = total.astype(BF16)
        x_send[c] = plane
        x_recv[c, x] = plane
        for d in range(1, NX):
            x_copy(c, d).start()
        for d in range(1, NX):
            s = lax.rem(x + d, NX)
            arrival(x_recv.at[c, s], x_rsem.at[c, s], {"ctx": x_device(d)}).wait_recv()
        running = base[...]
        for s in range(NX):
            running = running + jnp.where(s < x, x_recv[c, s].astype(F32), 0.0)
        for s in range(NZ):
            prefix_send[c, s] = running.astype(BF16)
            running = running + state_recv[c, s].astype(F32)
        prefix_recv[c, z] = prefix_send[c, z]
        for d in ORDER:
            prefix_copy(c, d).start()

    loads[4].wait()
    peer = 1 - core

    def att_copy(h):
        cols = pl.ds(pl.multiple_of(core * width + h * dh, dh), dh)
        return pltpu.make_async_remote_copy(
            src_ref=att.at[peer, :, cols], dst_ref=att.at[peer, :, cols],
            send_sem=a_ssem.at[h], recv_sem=a_rsem.at[h],
            device_id={"head": peer}, device_id_type=MESH,
        )

    def last_head(h):
        cols = head_columns(h)
        gain = gain_ref[:, cols].astype(F32)
        for b in (peer, core):
            span = pl.ds(pl.multiple_of(b * BLK, BLK), BLK)
            numerator = local[span, cols]
            for c in range(CHUNKS):
                numerator = numerator + dot(
                    qf[h, span, c * part : (c + 1) * part], prefix_recv[c, h]
                )
            mean = jnp.mean(numerator * numerator, axis=-1, keepdims=True)
            att[b, :, pl.ds(pl.multiple_of(core * width + h * dh, dh), dh)] = (
                numerator * lax.rsqrt(mean + EPSILON) * gain
            ).astype(BF16)
        att_copy(h).start()

    last_head(z)

    def last_step(i, carry):
        d = lax.select(i % 2 == 0, 1 + i // 2, NZ - 1 - i // 2)
        h = at_z(d)
        for c in range(CHUNKS):
            arrival(prefix_recv.at[c, h], p_rsem.at[c, h], {"ctx": z_device(d)}).wait_recv()
        last_head(h)
        return carry

    lax.fori_loop(0, NZ - 1, last_step, 0)

    loads[5].wait()
    w_copy.wait()
    for h in range(heads):
        cols = pl.ds(pl.multiple_of(peer * width + h * dh, dh), dh)
        arrival(att.at[core, :, cols], a_rsem.at[h], {"head": peer}).wait_recv()
    columns = w_ref.shape[1]
    tile = columns // OUT_TILES

    def out_copy(n):
        cols = pl.ds(pl.multiple_of(n * tile, tile), tile)
        return pltpu.make_async_copy(out_ref.at[:, cols], out_hbm.at[:, cols], out_sem.at[n])

    def out_step(n, carry):
        cols = pl.ds(pl.multiple_of(n * tile, tile), tile)
        out_ref[:, cols] = dot(att[core], w_ref[:, cols]).astype(BF16)
        out_copy(n).start()
        return carry

    lax.fori_loop(0, OUT_TILES, out_step, 0)

    for h in range(heads):
        att_copy(h).wait_send()
    for c in range(CHUNKS):
        for d in ORDER:
            state_copy(c, d).wait_send()
            prefix_copy(c, d).wait_send()
        for d in range(1, NY):
            y_copy(c, d).wait_send()
        for d in range(1, NX):
            x_copy(c, d).wait_send()
    for n in range(OUT_TILES):
        out_copy(n).wait()


def local(queries, key_vectors, values, features, norm_gain, out_weight):
    heads, dh, m = features.shape
    rows, width = queries.shape
    full, columns = 2 * width, out_weight.shape[1]
    part = m // CHUNKS
    dma = pltpu.SemaphoreType.DMA
    return pl.pallas_call(
        kernel,
        out_shape=jax.ShapeDtypeStruct((rows // 2, columns), BF16),
        in_specs=[pl.BlockSpec(memory_space=pl.ANY)] * 6,
        out_specs=pl.BlockSpec(memory_space=pl.ANY),
        scratch_shapes=[
            pltpu.VMEM((rows, width), BF16),
            pltpu.VMEM((rows, width), BF16),
            pltpu.VMEM((rows, width), BF16),
            pltpu.VMEM((heads, dh, m), BF16),
            pltpu.VMEM((1, width), BF16),
            pltpu.VMEM((full, columns), BF16),
            pltpu.VMEM((rows // 2, columns), BF16),
            pltpu.VMEM((heads, m, rows), BF16),
            pltpu.VMEM((heads, rows, m), BF16),
            pltpu.VMEM((rows, width), F32),
            pltpu.VMEM((heads, m, dh), BF16),
            pltpu.VMEM((CHUNKS, NZ, part, dh), BF16),
            pltpu.VMEM((CHUNKS, NZ, part, dh), BF16),
            pltpu.VMEM((CHUNKS, part, dh), BF16),
            pltpu.VMEM((CHUNKS, NY, part, dh), BF16),
            pltpu.VMEM((CHUNKS, part, dh), BF16),
            pltpu.VMEM((CHUNKS, NX, part, dh), BF16),
            pltpu.VMEM((CHUNKS, NZ, part, dh), BF16),
            pltpu.VMEM((CHUNKS, NZ, part, dh), BF16),
            pltpu.VMEM((2, rows // 2, full), BF16),
            pltpu.VMEM((part, dh), F32),
            dma((6,)),
            dma((OUT_TILES,)),
            dma((2,)),
            dma((CHUNKS, NZ)),
            dma((CHUNKS, NZ)),
            dma((CHUNKS, NY)),
            dma((CHUNKS, NY)),
            dma((CHUNKS, NX)),
            dma((CHUNKS, NX)),
            dma((CHUNKS, NZ)),
            dma((CHUNKS, NZ)),
            dma((heads,)),
            dma((heads,)),
        ],
        compiler_params=pltpu.CompilerParams(
            collective_id=0, has_side_effects=True, vmem_limit_bytes=60 * 1024 * 1024
        ),
        cost_estimate=pl.CostEstimate(flops=4 * 10**9, bytes_accessed=10**7, transcendentals=2 * 10**6),
    )(queries, key_vectors, values, features, norm_gain.reshape(1, width), out_weight)


def solution(mesh):
    return jax.shard_map(
        local,
        mesh=mesh,
        in_specs=(
            P("ctx", "head"),
            P("ctx", "head"),
            P("ctx", "head"),
            P("head", None, None),
            P("head"),
            P("head", None),
        ),
        out_specs=P(("ctx", "head"), None),
        check_vma=False,
    )
```

```python
import jax
import jax.numpy as jnp
from jax import lax
from jax.experimental import pallas as pl
from jax.experimental.pallas import tpu as pltpu
from jax.sharding import PartitionSpec as P

MESH = pl.DeviceIdType.MESH
F32 = jnp.float32
BF16 = jnp.bfloat16
BLK = 256
NX, NY, NZ = 4, 4, 8
NXY = NX * NY
CHUNKS = 4
OUT_TILES = 4
EPSILON = 1e-05
ORDER = (4, 3, 5, 2, 6, 1, 7)


def dot(a, b, contract=((1,), (0,))):
    return lax.dot_general(a, b, (contract, ((), ())), preferred_element_type=F32)


def halves(squared):
    high = squared.astype(BF16)
    return high, (squared - high.astype(F32)).astype(BF16)


def kernel(
    q_hbm, k_hbm, v_hbm, f_hbm, gain_hbm, w_hbm, out_ref,
    q_ref, k_ref, v_ref, f_ref, gain_ref, w_ref, kft, qf, local, first,
    state_send, state_recv, line_send, line_recv, prefix_send, prefix_recv, att, gains, acc,
    load_sem, w_sems, s_ssem, s_rsem, l_ssem, l_rsem, p_ssem, p_rsem, a_ssem, a_rsem,
):
    heads, dh, m = f_ref.shape
    rows = q_ref.shape[0]
    width = heads * dh
    per = heads // CHUNKS
    piece = m // NZ
    scale = dh ** (-0.25)
    log2e = 1.4426950408889634
    shift = 0.5 * (m.bit_length() - 1)
    me = lax.axis_index("ctx")
    core = lax.axis_index("head")
    peer = 1 - core
    z = lax.rem(me, NZ)
    w = me // NZ

    def at_z(d):
        return lax.rem(z + d, NZ)

    def z_device(d):
        return {"ctx": me - z + at_z(d)}

    def head_columns(h):
        return pl.ds(pl.multiple_of(h * dh, dh), dh)

    def heads_of(c):
        return pl.ds(c * per, per)

    def piece_of(s):
        return pl.ds(pl.multiple_of(s * piece, piece), piece)

    own_rows = pl.ds(pl.multiple_of(core * width, width), width)

    loads = [
        pltpu.make_async_copy(src, dst, load_sem.at[i])
        for i, (src, dst) in enumerate(
            (
                (f_hbm, f_ref),
                (k_hbm, k_ref),
                (v_hbm, v_ref),
                (q_hbm, q_ref),
                (gain_hbm, gain_ref),
                (w_hbm, w_ref.at[own_rows, :]),
            )
        )
    ]
    for load in loads:
        load.start()

    barrier = pltpu.get_barrier_semaphore()
    for d in range(1, NZ):
        pl.semaphore_signal(barrier, inc=1, device_id=z_device(d), device_id_type=MESH)
    for d in range(1, NXY):
        pl.semaphore_signal(
            barrier, inc=1, device_id={"ctx": lax.rem(w + d, NXY) * NZ + z}, device_id_type=MESH
        )
    pl.semaphore_signal(barrier, inc=1, device_id={"head": peer}, device_id_type=MESH)
    pl.semaphore_wait(barrier, NZ - 1 + NXY - 1 + 1)

    w_copy = pltpu.make_async_remote_copy(
        src_ref=w_hbm, dst_ref=w_ref.at[own_rows, :], send_sem=w_sems.at[0], recv_sem=w_sems.at[1],
        device_id={"head": peer}, device_id_type=MESH,
    )
    w_copy.start()

    def state_copy(c, d):
        return pltpu.make_async_remote_copy(
            src_ref=state_send.at[heads_of(c), piece_of(at_z(d))], dst_ref=state_recv.at[c, z],
            send_sem=s_ssem.at[c, d], recv_sem=s_rsem.at[c, z],
            device_id=z_device(d), device_id_type=MESH,
        )

    def line_copy(c, t):
        return pltpu.make_async_remote_copy(
            src_ref=line_send.at[c], dst_ref=line_recv.at[c, w],
            send_sem=l_ssem.at[c, t], recv_sem=l_rsem.at[c, w],
            device_id={"ctx": t * NZ + z}, device_id_type=MESH,
        )

    def prefix_copy(c, d):
        return pltpu.make_async_remote_copy(
            src_ref=prefix_send.at[c, at_z(d)], dst_ref=prefix_recv.at[heads_of(c), piece_of(z)],
            send_sem=p_ssem.at[c, d], recv_sem=p_rsem.at[c, z],
            device_id=z_device(d), device_id_type=MESH,
        )

    def att_columns(owner, c):
        return pl.ds(pl.multiple_of(owner * width + c * (per * dh), per * dh), per * dh)

    def att_copy(c):
        cols = att_columns(core, c)
        return pltpu.make_async_remote_copy(
            src_ref=att.at[peer, :, cols], dst_ref=att.at[peer, :, cols],
            send_sem=a_ssem.at[c], recv_sem=a_rsem.at[c],
            device_id={"head": peer}, device_id_type=MESH,
        )

    def arrival(ref, sem, device_id):
        return pltpu.make_async_remote_copy(
            src_ref=ref, dst_ref=ref, send_sem=sem, recv_sem=sem, device_id=device_id, device_id_type=MESH
        )

    loads[0].wait()
    loads[1].wait()
    loads[2].wait()
    ones_row = jnp.ones((8, dh), BF16)

    def key_head(h):
        cols = head_columns(h)
        k = k_ref[:, cols]
        v = v_ref[:, cols]
        linear = dot(f_ref[h].T, k, ((1,), (1,)))
        wide = k.astype(F32)
        high, low = halves(wide * wide)
        squares = (dot(ones_row, high, ((1,), (1,))) + dot(ones_row, low, ((1,), (1,))))[0:1]
        feats = jnp.exp2(
            linear * (scale * log2e) - (squares * (0.5 * scale * scale * log2e) + shift)
        ).astype(BF16)
        kft[h] = feats
        one = dot(feats[:, :BLK], v[:BLK])
        two = dot(feats[:, BLK:], v[BLK:])
        first[h] = one.astype(BF16)
        state_send[h] = (one + two).astype(BF16)

    def key_chunk(c, carry):
        for i in range(per):
            key_head(c * per + i)
        for d in ORDER:
            state_copy(c, d).start()
        state_recv[c, z] = state_send[heads_of(c), piece_of(z)]
        return carry

    lax.fori_loop(0, CHUNKS, key_chunk, 0)

    loads[3].wait()
    ones_square = jnp.ones((dh, dh), BF16)
    mask = lax.broadcasted_iota(jnp.int32, (BLK, BLK), 0) >= lax.broadcasted_iota(jnp.int32, (BLK, BLK), 1)

    def query_head(h, carry):
        cols = head_columns(h)
        q = q_ref[:, cols]
        wide = q.astype(F32)
        high, low = halves(wide * wide)
        squares = dot(high, ones_square) + dot(low, ones_square)
        away = squares * (0.5 * scale * scale * log2e) + shift
        linear = dot(q, f_ref[h])
        feats = jnp.exp2(
            linear * (scale * log2e) - jnp.concatenate([away] * (m // dh), axis=1)
        ).astype(BF16)
        qf[h] = feats
        for b in range(rows // BLK):
            span = slice(b * BLK, (b + 1) * BLK)
            scores = dot(feats[span], kft[h, :, span])
            weights = jnp.where(mask, scores, 0.0).astype(BF16)
            term = dot(weights, v_ref[span, cols])
            if b > 0:
                term = term + dot(feats[span], first[h])
            local[span, cols] = term
        return carry

    def query_chunk(c):
        lax.fori_loop(c * per, (c + 1) * per, query_head, 0)

    def line_sum(c):
        for d in range(1, NZ):
            s = at_z(d)
            arrival(state_recv.at[c, s], s_rsem.at[c, s], z_device(d)).wait_recv()
        total = jnp.zeros((per, piece, dh), F32)
        for s in range(NZ):
            total = total + state_recv[c, s].astype(F32)
        line_send[c] = total.astype(BF16)

        def send(t, carry):
            line_copy(c, t).start()
            return carry

        lax.fori_loop(w + 1, NXY, send, 0)

    def prefixes(c):
        def one(s, running):
            arrival(line_recv.at[c, s], l_rsem.at[c, s], {"ctx": s * NZ + z}).wait_recv()
            return running + line_recv[c, s].astype(F32)

        running = lax.fori_loop(0, w, one, jnp.zeros((per, piece, dh), F32))
        for s in range(NZ):
            prefix_send[c, s] = running.astype(BF16)
            running = running + state_recv[c, s].astype(F32)
        for d in ORDER:
            prefix_copy(c, d).start()
        prefix_recv[heads_of(c), piece_of(z)] = prefix_send[c, z]

    def last_chunk(c):
        for d in range(1, NZ):
            s = at_z(d)
            arrival(prefix_recv.at[heads_of(c), piece_of(s)], p_rsem.at[c, s], z_device(d)).wait_recv()
        for b in (peer, core):
            span = pl.ds(pl.multiple_of(b * BLK, BLK), BLK)
            for i in range(per):
                h = c * per + i
                numerator = local[span, head_columns(h)] + dot(qf[h, span], prefix_recv[h])
                mean = jnp.mean(numerator * numerator, axis=-1, keepdims=True)
                att[b, :, pl.ds(pl.multiple_of(core * width + h * dh, dh), dh)] = (
                    numerator * lax.rsqrt(mean + EPSILON) * gains[h : h + 1, :]
                ).astype(BF16)
            if b is peer:
                att_copy(c).start()

    def att_wait(c):
        cols = att_columns(peer, c)
        arrival(att.at[core, :, cols], a_rsem.at[c], {"head": peer}).wait_recv()

    tile = w_ref.shape[1] // OUT_TILES

    def project(blocks, start, end):
        def one(n, carry):
            cols = pl.ds(pl.multiple_of(n * tile, tile), tile)
            total = None if start else acc[:, cols]
            for block in blocks:
                product = dot(att[core, :, block], w_ref[block, cols])
                total = product if total is None else total + product
            if end:
                out_ref[:, cols] = total.astype(BF16)
            else:
                acc[:, cols] = total
            return carry

        lax.fori_loop(0, OUT_TILES, one, 0)

    query_chunk(0)
    query_chunk(1)
    line_sum(0)
    query_chunk(2)
    line_sum(1)
    query_chunk(3)
    loads[4].wait()
    wide_gain = gain_ref[...].astype(F32)
    for h in range(heads):
        gains[h : h + 1, :] = wide_gain[h * dh : (h + 1) * dh].reshape(1, dh)
    line_sum(2)
    prefixes(0)
    line_sum(3)
    prefixes(1)
    prefixes(2)
    prefixes(3)
    loads[5].wait()
    w_copy.wait()
    for c in range(CHUNKS):
        last_chunk(c)
        if c == 0:
            project([att_columns(core, c)], True, False)
        else:
            att_wait(c - 1)
            project([att_columns(core, c), att_columns(peer, c - 1)], False, False)
    att_wait(CHUNKS - 1)
    project([att_columns(peer, CHUNKS - 1)], False, True)

    for c in range(CHUNKS):
        att_copy(c).wait_send()
        for d in ORDER:
            state_copy(c, d).wait_send()
            prefix_copy(c, d).wait_send()

        def sent(t, carry):
            line_copy(c, t).wait_send()
            return carry

        lax.fori_loop(w + 1, NXY, sent, 0)


def attention(queries, key_vectors, values, features, norm_gain, out_weight):
    heads, dh, m = features.shape
    rows, width = queries.shape
    full, columns = 2 * width, out_weight.shape[1]
    slab = (heads // CHUNKS, m // NZ, dh)
    dma = pltpu.SemaphoreType.DMA
    return pl.pallas_call(
        kernel,
        out_shape=pltpu.VMEM((rows // 2, columns), BF16),
        in_specs=[pl.BlockSpec(memory_space=pl.ANY)] * 6,
        out_specs=pl.BlockSpec(memory_space=pltpu.VMEM),
        scratch_shapes=[
            pltpu.VMEM((rows, width), BF16),
            pltpu.VMEM((rows, width), BF16),
            pltpu.VMEM((rows, width), BF16),
            pltpu.VMEM((heads, dh, m), BF16),
            pltpu.VMEM((width,), BF16),
            pltpu.VMEM((full, columns), BF16),
            pltpu.VMEM((heads, m, rows), BF16),
            pltpu.VMEM((heads, rows, m), BF16),
            pltpu.VMEM((rows, width), F32),
            pltpu.VMEM((heads, m, dh), BF16),
            pltpu.VMEM((heads, m, dh), BF16),
            pltpu.VMEM((CHUNKS, NZ) + slab, BF16),
            pltpu.VMEM((CHUNKS,) + slab, BF16),
            pltpu.VMEM((CHUNKS, NXY) + slab, BF16),
            pltpu.VMEM((CHUNKS, NZ) + slab, BF16),
            pltpu.VMEM((heads, m, dh), BF16),
            pltpu.VMEM((2, rows // 2, full), BF16),
            pltpu.VMEM((heads, dh), F32),
            pltpu.VMEM((rows // 2, columns), F32),
            dma((6,)),
            dma((2,)),
            dma((CHUNKS, NZ)),
            dma((CHUNKS, NZ)),
            dma((CHUNKS, NXY)),
            dma((CHUNKS, NXY)),
            dma((CHUNKS, NZ)),
            dma((CHUNKS, NZ)),
            dma((CHUNKS,)),
            dma((CHUNKS,)),
        ],
        compiler_params=pltpu.CompilerParams(
            collective_id=0, has_side_effects=True, vmem_limit_bytes=60 * 1024 * 1024
        ),
        cost_estimate=pl.CostEstimate(flops=4 * 10**9, bytes_accessed=10**7, transcendentals=2 * 10**6),
    )(queries, key_vectors, values, features, norm_gain, out_weight)


def solution(mesh):
    return jax.shard_map(
        attention,
        mesh=mesh,
        in_specs=(
            P("ctx", "head"),
            P("ctx", "head"),
            P("ctx", "head"),
            P("head", None, None),
            P("head"),
            P("head", None),
        ),
        out_specs=P(("ctx", "head"), None),
        check_vma=False,
    )
```

```python
import jax
import jax.numpy as jnp
from jax import lax
from jax.experimental import pallas as pl
from jax.experimental.pallas import tpu as pltpu
from jax.sharding import PartitionSpec as P

MESH = pl.DeviceIdType.MESH
F32 = jnp.float32
BF16 = jnp.bfloat16
BLK = 256
NX, NY, NZ = 4, 4, 8
NXY = NX * NY
SIZES = (2, 2, 2, 2)
CHUNKS = len(SIZES)
STARTS = tuple(sum(SIZES[:c]) for c in range(CHUNKS))
SCHEDULE = (
    ("line", 0, 2),
    ("line", 1, 1),
    ("line", 2, 1),
    ("prefix", 0, 0),
    ("line", 3, 0),
    ("prefix", 1, 0),
    ("prefix", 2, 0),
    ("prefix", 3, 0),
)
OUT_TILES = 4
EPSILON = 1e-05
ORDER = (4, 3, 5, 2, 6, 1, 7)


def dot(a, b, contract=((1,), (0,))):
    return lax.dot_general(a, b, (contract, ((), ())), preferred_element_type=F32)


def halves(squared):
    high = squared.astype(BF16)
    return high, (squared - high.astype(F32)).astype(BF16)


def kernel(
    q_hbm, k_hbm, v_hbm, f_hbm, gain_hbm, w_hbm, out_ref,
    q_ref, k_ref, v_ref, f_ref, gain_ref, w_ref, kft, qf, local, first,
    state_send, state_recv, line_send, line_recv, prefix_send, prefix_recv, att, gains, acc,
    load_sem, kv_sems, w_sems, s_ssem, s_rsem, l_ssem, l_rsem, p_ssem, p_rsem, a_ssem, a_rsem,
):
    heads, dh, m = f_ref.shape
    rows = q_ref.shape[0]
    width = heads * dh
    piece = m // NZ
    scale = dh ** (-0.25)
    log2e = 1.4426950408889634
    shift = 0.5 * (m.bit_length() - 1)
    me = lax.axis_index("ctx")
    core = lax.axis_index("head")
    peer = 1 - core
    z = lax.rem(me, NZ)
    w = me // NZ

    def at_z(d):
        return lax.rem(z + d, NZ)

    def z_device(d):
        return {"ctx": me - z + at_z(d)}

    def head_columns(h):
        return pl.ds(pl.multiple_of(h * dh, dh), dh)

    def heads_of(c):
        return pl.ds(STARTS[c], SIZES[c])

    def piece_of(s):
        return pl.ds(pl.multiple_of(s * piece, piece), piece)

    own_rows = pl.ds(pl.multiple_of(core * width, width), width)

    def chunk_load(i, c):
        src, dst = ((k_hbm, k_ref), (v_hbm, v_ref))[i]
        cols = pl.ds(STARTS[c] * dh, SIZES[c] * dh)
        return pltpu.make_async_copy(src.at[:, cols], dst.at[:, cols], kv_sems.at[i, c])

    loads = [
        pltpu.make_async_copy(src, dst, load_sem.at[i])
        for i, (src, dst) in enumerate(
            ((f_hbm, f_ref), (q_hbm, q_ref), (gain_hbm, gain_ref), (w_hbm, w_ref.at[own_rows, :]))
        )
    ]
    loads[0].start()
    for c in range(CHUNKS):
        chunk_load(0, c).start()
        chunk_load(1, c).start()

    barrier = pltpu.get_barrier_semaphore()
    for d in range(1, NZ):
        pl.semaphore_signal(barrier, inc=1, device_id=z_device(d), device_id_type=MESH)
    for d in range(1, NXY):
        pl.semaphore_signal(
            barrier, inc=1, device_id={"ctx": lax.rem(w + d, NXY) * NZ + z}, device_id_type=MESH
        )
    pl.semaphore_signal(barrier, inc=1, device_id={"head": peer}, device_id_type=MESH)

    w_copy = pltpu.make_async_remote_copy(
        src_ref=w_hbm, dst_ref=w_ref.at[own_rows, :], send_sem=w_sems.at[0], recv_sem=w_sems.at[1],
        device_id={"head": peer}, device_id_type=MESH,
    )

    def state_copy(c, d):
        return pltpu.make_async_remote_copy(
            src_ref=state_send.at[heads_of(c), piece_of(at_z(d))], dst_ref=state_recv.at[z, heads_of(c)],
            send_sem=s_ssem.at[c, d], recv_sem=s_rsem.at[c, z],
            device_id=z_device(d), device_id_type=MESH,
        )

    def line_copy(c, t):
        return pltpu.make_async_remote_copy(
            src_ref=line_send.at[heads_of(c)], dst_ref=line_recv.at[w, heads_of(c)],
            send_sem=l_ssem.at[c, t], recv_sem=l_rsem.at[c, w],
            device_id={"ctx": t * NZ + z}, device_id_type=MESH,
        )

    def prefix_copy(c, d):
        return pltpu.make_async_remote_copy(
            src_ref=prefix_send.at[at_z(d), heads_of(c)], dst_ref=prefix_recv.at[heads_of(c), piece_of(z)],
            send_sem=p_ssem.at[c, d], recv_sem=p_rsem.at[c, z],
            device_id=z_device(d), device_id_type=MESH,
        )

    def att_columns(owner, c):
        return pl.ds(pl.multiple_of(owner * width + STARTS[c] * dh, dh), SIZES[c] * dh)

    def att_copy(c):
        cols = att_columns(core, c)
        return pltpu.make_async_remote_copy(
            src_ref=att.at[peer, :, cols], dst_ref=att.at[peer, :, cols],
            send_sem=a_ssem.at[c], recv_sem=a_rsem.at[c],
            device_id={"head": peer}, device_id_type=MESH,
        )

    def arrival(ref, sem, device_id):
        return pltpu.make_async_remote_copy(
            src_ref=ref, dst_ref=ref, send_sem=sem, recv_sem=sem, device_id=device_id, device_id_type=MESH
        )

    loads[0].wait()
    ones_row = jnp.ones((8, dh), BF16)

    def key_head(h):
        cols = head_columns(h)
        k = k_ref[:, cols]
        v = v_ref[:, cols]
        linear = dot(f_ref[h].T, k, ((1,), (1,)))
        wide = k.astype(F32)
        high, low = halves(wide * wide)
        squares = (dot(ones_row, high, ((1,), (1,))) + dot(ones_row, low, ((1,), (1,))))[0:1]
        feats = jnp.exp2(
            linear * (scale * log2e) - (squares * (0.5 * scale * scale * log2e) + shift)
        ).astype(BF16)
        kft[h] = feats
        one = dot(feats[:, :BLK], v[:BLK])
        two = dot(feats[:, BLK:], v[BLK:])
        first[h] = one.astype(BF16)
        state_send[h] = (one + two).astype(BF16)

    for c in range(CHUNKS):
        chunk_load(0, c).wait()
        chunk_load(1, c).wait()
        for i in range(SIZES[c]):
            key_head(STARTS[c] + i)
        if c == 0:
            pl.semaphore_wait(barrier, NZ - 1 + NXY - 1 + 1)
        for d in ORDER:
            state_copy(c, d).start()
        state_recv[z, heads_of(c)] = state_send[heads_of(c), piece_of(z)]
        if c == 0:
            for load in loads[1:]:
                load.start()
            w_copy.start()

    loads[1].wait()
    ones_square = jnp.ones((dh, dh), BF16)
    mask = lax.broadcasted_iota(jnp.int32, (BLK, BLK), 0) >= lax.broadcasted_iota(jnp.int32, (BLK, BLK), 1)

    def query_head(h, carry):
        cols = head_columns(h)
        q = q_ref[:, cols]
        wide = q.astype(F32)
        high, low = halves(wide * wide)
        squares = dot(high, ones_square) + dot(low, ones_square)
        away = squares * (0.5 * scale * scale * log2e) + shift
        linear = dot(q, f_ref[h])
        feats = jnp.exp2(
            linear * (scale * log2e) - jnp.concatenate([away] * (m // dh), axis=1)
        ).astype(BF16)
        qf[h] = feats
        for b in range(rows // BLK):
            span = slice(b * BLK, (b + 1) * BLK)
            scores = dot(feats[span], kft[h, :, span])
            weights = jnp.where(mask, scores, 0.0).astype(BF16)
            term = dot(weights, v_ref[span, cols])
            if b > 0:
                term = term + dot(feats[span], first[h])
            local[span, cols] = term
        return carry

    def query_chunk(c):
        lax.fori_loop(STARTS[c], STARTS[c] + SIZES[c], query_head, 0)

    def line_sum(c):
        for d in range(1, NZ):
            s = at_z(d)
            arrival(state_recv.at[s, heads_of(c)], s_rsem.at[c, s], z_device(d)).wait_recv()
        total = jnp.zeros((SIZES[c], piece, dh), F32)
        for s in range(NZ):
            total = total + state_recv[s, heads_of(c)].astype(F32)
        line_send[heads_of(c)] = total.astype(BF16)

        def send(t, carry):
            line_copy(c, t).start()
            return carry

        lax.fori_loop(w + 1, NXY, send, 0)

    def prefixes(c):
        def one(s, running):
            arrival(line_recv.at[s, heads_of(c)], l_rsem.at[c, s], {"ctx": s * NZ + z}).wait_recv()
            return running + line_recv[s, heads_of(c)].astype(F32)

        running = lax.fori_loop(0, w, one, jnp.zeros((SIZES[c], piece, dh), F32))
        for s in range(NZ):
            prefix_send[s, heads_of(c)] = running.astype(BF16)
            running = running + state_recv[s, heads_of(c)].astype(F32)
        for d in ORDER:
            prefix_copy(c, d).start()
        prefix_recv[heads_of(c), piece_of(z)] = prefix_send[z, heads_of(c)]

    def last_chunk(c):
        for d in range(1, NZ):
            s = at_z(d)
            arrival(prefix_recv.at[heads_of(c), piece_of(s)], p_rsem.at[c, s], z_device(d)).wait_recv()
        for b in (peer, core):
            span = pl.ds(pl.multiple_of(b * BLK, BLK), BLK)
            for i in range(SIZES[c]):
                h = STARTS[c] + i
                numerator = local[span, head_columns(h)] + dot(qf[h, span], prefix_recv[h])
                mean = jnp.mean(numerator * numerator, axis=-1, keepdims=True)
                att[b, :, pl.ds(pl.multiple_of(core * width + h * dh, dh), dh)] = (
                    numerator * lax.rsqrt(mean + EPSILON) * gains[h : h + 1, :]
                ).astype(BF16)
            if b is peer:
                att_copy(c).start()

    def att_wait(c):
        cols = att_columns(peer, c)
        arrival(att.at[core, :, cols], a_rsem.at[c], {"head": peer}).wait_recv()

    tile = w_ref.shape[1] // OUT_TILES

    def project(blocks, start, end):
        def one(n, carry):
            cols = pl.ds(pl.multiple_of(n * tile, tile), tile)
            total = None if start else acc[:, cols]
            for block in blocks:
                product = dot(att[core, :, block], w_ref[block, cols])
                total = product if total is None else total + product
            if end:
                out_ref[:, cols] = total.astype(BF16)
            else:
                acc[:, cols] = total
            return carry

        lax.fori_loop(0, OUT_TILES, one, 0)

    waiting = list(range(CHUNKS))
    for name, c, queries in SCHEDULE:
        for _ in range(queries):
            query_chunk(waiting.pop(0))
        if name == "line":
            line_sum(c)
        else:
            prefixes(c)
    loads[2].wait()
    wide_gain = gain_ref[...].astype(F32)
    for h in range(heads):
        gains[h : h + 1, :] = wide_gain[h * dh : (h + 1) * dh].reshape(1, dh)
    loads[3].wait()
    w_copy.wait()

    for c in range(CHUNKS):
        for d in ORDER:
            state_copy(c, d).wait_send()

        def sent(t, carry):
            line_copy(c, t).wait_send()
            return carry

        lax.fori_loop(w + 1, NXY, sent, 0)

    for c in range(CHUNKS):
        last_chunk(c)
        if c > 0:
            att_copy(c - 1).wait_send()
        if c == 0:
            project([att_columns(core, c)], True, False)
        else:
            att_wait(c - 1)
            project([att_columns(core, c), att_columns(peer, c - 1)], False, False)
    for c in range(CHUNKS):
        for d in ORDER:
            prefix_copy(c, d).wait_send()
    att_wait(CHUNKS - 1)
    project([att_columns(peer, CHUNKS - 1)], False, True)

    att_copy(CHUNKS - 1).wait_send()


def attention(queries, key_vectors, values, features, norm_gain, out_weight):
    heads, dh, m = features.shape
    rows, width = queries.shape
    full, columns = 2 * width, out_weight.shape[1]
    slab = (heads, m // NZ, dh)
    dma = pltpu.SemaphoreType.DMA
    return pl.pallas_call(
        kernel,
        out_shape=pltpu.VMEM((rows // 2, columns), BF16),
        in_specs=[pl.BlockSpec(memory_space=pl.ANY)] * 6,
        out_specs=pl.BlockSpec(memory_space=pltpu.VMEM),
        scratch_shapes=[
            pltpu.VMEM((rows, width), BF16),
            pltpu.VMEM((rows, width), BF16),
            pltpu.VMEM((rows, width), BF16),
            pltpu.VMEM((heads, dh, m), BF16),
            pltpu.VMEM((width,), BF16),
            pltpu.VMEM((full, columns), BF16),
            pltpu.VMEM((heads, m, rows), BF16),
            pltpu.VMEM((heads, rows, m), BF16),
            pltpu.VMEM((rows, width), F32),
            pltpu.VMEM((heads, m, dh), BF16),
            pltpu.VMEM((heads, m, dh), BF16),
            pltpu.VMEM((NZ,) + slab, BF16),
            pltpu.VMEM(slab, BF16),
            pltpu.VMEM((NXY,) + slab, BF16),
            pltpu.VMEM((NZ,) + slab, BF16),
            pltpu.VMEM((heads, m, dh), BF16),
            pltpu.VMEM((2, rows // 2, full), BF16),
            pltpu.VMEM((heads, dh), F32),
            pltpu.VMEM((rows // 2, columns), F32),
            dma((4,)),
            dma((2, CHUNKS)),
            dma((2,)),
            dma((CHUNKS, NZ)),
            dma((CHUNKS, NZ)),
            dma((CHUNKS, NXY)),
            dma((CHUNKS, NXY)),
            dma((CHUNKS, NZ)),
            dma((CHUNKS, NZ)),
            dma((CHUNKS,)),
            dma((CHUNKS,)),
        ],
        compiler_params=pltpu.CompilerParams(
            collective_id=0, has_side_effects=True, vmem_limit_bytes=60 * 1024 * 1024
        ),
        cost_estimate=pl.CostEstimate(flops=4 * 10**9, bytes_accessed=10**7, transcendentals=2 * 10**6),
    )(queries, key_vectors, values, features, norm_gain, out_weight)


def solution(mesh):
    return jax.shard_map(
        attention,
        mesh=mesh,
        in_specs=(
            P("ctx", "head"),
            P("ctx", "head"),
            P("ctx", "head"),
            P("head", None, None),
            P("head"),
            P("head", None),
        ),
        out_specs=P(("ctx", "head"), None),
        check_vma=False,
    )
```

```python
import jax
import jax.numpy as jnp
from jax import lax
from jax.experimental import pallas as pl
from jax.experimental.pallas import tpu as pltpu
from jax.sharding import PartitionSpec as P

MESH = pl.DeviceIdType.MESH
F32 = jnp.float32
BF16 = jnp.bfloat16
BLK = 256
NX, NY, NZ = 4, 4, 8
NXY = NX * NY
SIZES = (2, 2, 2, 2)
CHUNKS = len(SIZES)
STARTS = tuple(sum(SIZES[:c]) for c in range(CHUNKS))
SCHEDULE = (
    ("line", 0, 2),
    ("line", 1, 1),
    ("line", 2, 1),
    ("prefix", 0, 0),
    ("line", 3, 0),
    ("prefix", 1, 0),
    ("prefix", 2, 0),
    ("prefix", 3, 0),
)
OUT_TILES = 4
EPSILON = 1e-05
ORDER = (4, 3, 5, 2, 6, 1, 7)


def dot(a, b, contract=((1,), (0,))):
    return lax.dot_general(a, b, (contract, ((), ())), preferred_element_type=F32)


def halves(squared):
    high = squared.astype(BF16)
    return high, (squared - high.astype(F32)).astype(BF16)


def kernel(
    q_hbm, k_hbm, v_hbm, f_hbm, gain_hbm, w_hbm, out_ref,
    q_ref, k_ref, v_ref, f_ref, gain_ref, w_ref, kft, qf, local, first,
    state_send, state_recv, line_send, line_recv, prefix_send, prefix_recv, att, gains, acc,
    load_sem, kv_sems, w_sems, s_ssem, s_rsem, l_ssem, l_rsem, p_ssem, p_rsem, a_ssem, a_rsem,
):
    heads, dh, m = f_ref.shape
    rows = q_ref.shape[0]
    width = heads * dh
    piece = m // NZ
    scale = dh ** (-0.25)
    log2e = 1.4426950408889634
    shift = 0.5 * (m.bit_length() - 1)
    me = lax.axis_index("ctx")
    core = lax.axis_index("head")
    peer = 1 - core
    z = lax.rem(me, NZ)
    w = me // NZ

    def at_z(d):
        return lax.rem(z + d, NZ)

    def z_device(d):
        return {"ctx": me - z + at_z(d)}

    def head_columns(h):
        return pl.ds(pl.multiple_of(h * dh, dh), dh)

    def heads_of(c):
        return pl.ds(STARTS[c], SIZES[c])

    def piece_of(s):
        return pl.ds(pl.multiple_of(s * piece, piece), piece)

    own_rows = pl.ds(pl.multiple_of(core * width, width), width)

    def chunk_load(i, c):
        src, dst = ((k_hbm, k_ref), (v_hbm, v_ref))[i]
        cols = pl.ds(STARTS[c] * dh, SIZES[c] * dh)
        return pltpu.make_async_copy(src.at[:, cols], dst.at[:, cols], kv_sems.at[i, c])

    loads = [
        pltpu.make_async_copy(src, dst, load_sem.at[i])
        for i, (src, dst) in enumerate(
            ((f_hbm, f_ref), (q_hbm, q_ref), (gain_hbm, gain_ref), (w_hbm, w_ref.at[own_rows, :]))
        )
    ]
    loads[0].start()
    for c in range(CHUNKS):
        chunk_load(0, c).start()
        chunk_load(1, c).start()

    barrier = pltpu.get_barrier_semaphore()
    for d in range(1, NZ):
        pl.semaphore_signal(barrier, inc=1, device_id=z_device(d), device_id_type=MESH)
    for d in range(1, NXY):
        pl.semaphore_signal(
            barrier, inc=1, device_id={"ctx": lax.rem(w + d, NXY) * NZ + z}, device_id_type=MESH
        )
    pl.semaphore_signal(barrier, inc=1, device_id={"head": peer}, device_id_type=MESH)

    w_copy = pltpu.make_async_remote_copy(
        src_ref=w_hbm, dst_ref=w_ref.at[own_rows, :], send_sem=w_sems.at[0], recv_sem=w_sems.at[1],
        device_id={"head": peer}, device_id_type=MESH,
    )

    def state_copy(c, d):
        return pltpu.make_async_remote_copy(
            src_ref=state_send.at[heads_of(c), piece_of(at_z(d))], dst_ref=state_recv.at[z, heads_of(c)],
            send_sem=s_ssem.at[c], recv_sem=s_rsem.at[c],
            device_id=z_device(d), device_id_type=MESH,
        )

    def line_copy(c, t):
        return pltpu.make_async_remote_copy(
            src_ref=line_send.at[heads_of(c)], dst_ref=line_recv.at[w, heads_of(c)],
            send_sem=l_ssem.at[c, t], recv_sem=l_rsem.at[c, w],
            device_id={"ctx": t * NZ + z}, device_id_type=MESH,
        )

    def prefix_copy(c, d):
        return pltpu.make_async_remote_copy(
            src_ref=prefix_send.at[at_z(d), heads_of(c)], dst_ref=prefix_recv.at[heads_of(c), piece_of(z)],
            send_sem=p_ssem.at[c], recv_sem=p_rsem.at[c],
            device_id=z_device(d), device_id_type=MESH,
        )

    def att_columns(owner, c):
        return pl.ds(pl.multiple_of(owner * width + STARTS[c] * dh, dh), SIZES[c] * dh)

    def att_copy(c):
        cols = att_columns(core, c)
        return pltpu.make_async_remote_copy(
            src_ref=att.at[peer, :, cols], dst_ref=att.at[peer, :, cols],
            send_sem=a_ssem.at[c], recv_sem=a_rsem.at[c],
            device_id={"head": peer}, device_id_type=MESH,
        )

    def arrival(ref, sem, device_id):
        return pltpu.make_async_remote_copy(
            src_ref=ref, dst_ref=ref, send_sem=sem, recv_sem=sem, device_id=device_id, device_id_type=MESH
        )

    def all_pieces(c, send_sem, recv_sem):
        ref = prefix_recv.at[heads_of(c), pl.ds(0, (NZ - 1) * piece)]
        return pltpu.make_async_remote_copy(
            src_ref=ref, dst_ref=ref, send_sem=send_sem.at[c], recv_sem=recv_sem.at[c],
            device_id=z_device(1), device_id_type=MESH,
        )

    loads[0].wait()
    ones_row = jnp.ones((8, dh), BF16)

    def key_head(h):
        cols = head_columns(h)
        k = k_ref[:, cols]
        v = v_ref[:, cols]
        linear = dot(f_ref[h].T, k, ((1,), (1,)))
        wide = k.astype(F32)
        high, low = halves(wide * wide)
        squares = (dot(ones_row, high, ((1,), (1,))) + dot(ones_row, low, ((1,), (1,))))[0:1]
        feats = jnp.exp2(
            linear * (scale * log2e) - (squares * (0.5 * scale * scale * log2e) + shift)
        ).astype(BF16)
        kft[h] = feats
        one = dot(feats[:, :BLK], v[:BLK])
        two = dot(feats[:, BLK:], v[BLK:])
        first[h] = one.astype(BF16)
        state_send[h] = (one + two).astype(BF16)

    for c in range(CHUNKS):
        chunk_load(0, c).wait()
        chunk_load(1, c).wait()
        for i in range(SIZES[c]):
            key_head(STARTS[c] + i)
        if c == 0:
            pl.semaphore_wait(barrier, NZ - 1 + NXY - 1 + 1)
        for d in ORDER:
            state_copy(c, d).start()
        state_recv[z, heads_of(c)] = state_send[heads_of(c), piece_of(z)]
        if c == 0:
            for load in loads[1:]:
                load.start()
            w_copy.start()

    loads[1].wait()
    ones_square = jnp.ones((dh, dh), BF16)
    mask = lax.broadcasted_iota(jnp.int32, (BLK, BLK), 0) >= lax.broadcasted_iota(jnp.int32, (BLK, BLK), 1)

    def query_head(h, carry):
        cols = head_columns(h)
        q = q_ref[:, cols]
        wide = q.astype(F32)
        high, low = halves(wide * wide)
        squares = dot(high, ones_square) + dot(low, ones_square)
        away = squares * (0.5 * scale * scale * log2e) + shift
        linear = dot(q, f_ref[h])
        feats = jnp.exp2(
            linear * (scale * log2e) - jnp.concatenate([away] * (m // dh), axis=1)
        ).astype(BF16)
        qf[h] = feats
        for b in range(rows // BLK):
            span = slice(b * BLK, (b + 1) * BLK)
            scores = dot(feats[span], kft[h, :, span])
            weights = jnp.where(mask, scores, 0.0).astype(BF16)
            term = dot(weights, v_ref[span, cols])
            if b > 0:
                term = term + dot(feats[span], first[h])
            local[span, cols] = term
        return carry

    def query_chunk(c):
        lax.fori_loop(STARTS[c], STARTS[c] + SIZES[c], query_head, 0)

    def line_sum(c):
        all_pieces(c, s_ssem, s_rsem).wait_recv()
        total = jnp.zeros((SIZES[c], piece, dh), F32)
        for s in range(NZ):
            total = total + state_recv[s, heads_of(c)].astype(F32)
        line_send[heads_of(c)] = total.astype(BF16)

        def send(t, carry):
            line_copy(c, t).start()
            return carry

        lax.fori_loop(w + 1, NXY, send, 0)

    def prefixes(c):
        def one(s, running):
            arrival(line_recv.at[s, heads_of(c)], l_rsem.at[c, s], {"ctx": s * NZ + z}).wait_recv()
            return running + line_recv[s, heads_of(c)].astype(F32)

        running = lax.fori_loop(0, w, one, jnp.zeros((SIZES[c], piece, dh), F32))
        for s in range(NZ):
            prefix_send[s, heads_of(c)] = running.astype(BF16)
            running = running + state_recv[s, heads_of(c)].astype(F32)
        for d in ORDER:
            prefix_copy(c, d).start()
        prefix_recv[heads_of(c), piece_of(z)] = prefix_send[z, heads_of(c)]

    def last_chunk(c):
        all_pieces(c, p_ssem, p_rsem).wait_recv()
        for b in (peer, core):
            span = pl.ds(pl.multiple_of(b * BLK, BLK), BLK)
            for i in range(SIZES[c]):
                h = STARTS[c] + i
                numerator = local[span, head_columns(h)] + dot(qf[h, span], prefix_recv[h])
                mean = jnp.mean(numerator * numerator, axis=-1, keepdims=True)
                att[b, :, pl.ds(pl.multiple_of(core * width + h * dh, dh), dh)] = (
                    numerator * lax.rsqrt(mean + EPSILON) * gains[h : h + 1, :]
                ).astype(BF16)
            if b is peer:
                att_copy(c).start()

    def att_wait(c):
        cols = att_columns(peer, c)
        arrival(att.at[core, :, cols], a_rsem.at[c], {"head": peer}).wait_recv()

    tile = w_ref.shape[1] // OUT_TILES

    def project(blocks, start, end):
        def one(n, carry):
            cols = pl.ds(pl.multiple_of(n * tile, tile), tile)
            total = None if start else acc[:, cols]
            for block in blocks:
                product = dot(att[core, :, block], w_ref[block, cols])
                total = product if total is None else total + product
            if end:
                out_ref[:, cols] = total.astype(BF16)
            else:
                acc[:, cols] = total
            return carry

        lax.fori_loop(0, OUT_TILES, one, 0)

    waiting = list(range(CHUNKS))
    for name, c, queries in SCHEDULE:
        for _ in range(queries):
            query_chunk(waiting.pop(0))
        if name == "line":
            line_sum(c)
        else:
            prefixes(c)
    loads[2].wait()
    wide_gain = gain_ref[...].astype(F32)
    for h in range(heads):
        gains[h : h + 1, :] = wide_gain[h * dh : (h + 1) * dh].reshape(1, dh)
    loads[3].wait()
    w_copy.wait()

    for c in range(CHUNKS):
        all_pieces(c, s_ssem, s_rsem).wait_send()

        def sent(t, carry):
            line_copy(c, t).wait_send()
            return carry

        lax.fori_loop(w + 1, NXY, sent, 0)

    for c in range(CHUNKS):
        last_chunk(c)
        if c > 0:
            att_copy(c - 1).wait_send()
        if c == 0:
            project([att_columns(core, c)], True, False)
        else:
            att_wait(c - 1)
            project([att_columns(core, c), att_columns(peer, c - 1)], False, False)
    for c in range(CHUNKS):
        all_pieces(c, p_ssem, p_rsem).wait_send()
    att_wait(CHUNKS - 1)
    project([att_columns(peer, CHUNKS - 1)], False, True)

    att_copy(CHUNKS - 1).wait_send()


def attention(queries, key_vectors, values, features, norm_gain, out_weight):
    heads, dh, m = features.shape
    rows, width = queries.shape
    full, columns = 2 * width, out_weight.shape[1]
    slab = (heads, m // NZ, dh)
    dma = pltpu.SemaphoreType.DMA
    return pl.pallas_call(
        kernel,
        out_shape=pltpu.VMEM((rows // 2, columns), BF16),
        in_specs=[pl.BlockSpec(memory_space=pl.ANY)] * 6,
        out_specs=pl.BlockSpec(memory_space=pltpu.VMEM),
        scratch_shapes=[
            pltpu.VMEM((rows, width), BF16),
            pltpu.VMEM((rows, width), BF16),
            pltpu.VMEM((rows, width), BF16),
            pltpu.VMEM((heads, dh, m), BF16),
            pltpu.VMEM((width,), BF16),
            pltpu.VMEM((full, columns), BF16),
            pltpu.VMEM((heads, m, rows), BF16),
            pltpu.VMEM((heads, rows, m), BF16),
            pltpu.VMEM((rows, width), F32),
            pltpu.VMEM((heads, m, dh), BF16),
            pltpu.VMEM((heads, m, dh), BF16),
            pltpu.VMEM((NZ,) + slab, BF16),
            pltpu.VMEM(slab, BF16),
            pltpu.VMEM((NXY,) + slab, BF16),
            pltpu.VMEM((NZ,) + slab, BF16),
            pltpu.VMEM((heads, m, dh), BF16),
            pltpu.VMEM((2, rows // 2, full), BF16),
            pltpu.VMEM((heads, dh), F32),
            pltpu.VMEM((rows // 2, columns), F32),
            dma((4,)),
            dma((2, CHUNKS)),
            dma((2,)),
            dma((CHUNKS,)),
            dma((CHUNKS,)),
            dma((CHUNKS, NXY)),
            dma((CHUNKS, NXY)),
            dma((CHUNKS,)),
            dma((CHUNKS,)),
            dma((CHUNKS,)),
            dma((CHUNKS,)),
        ],
        compiler_params=pltpu.CompilerParams(
            collective_id=0, has_side_effects=True, vmem_limit_bytes=60 * 1024 * 1024
        ),
        cost_estimate=pl.CostEstimate(flops=4 * 10**9, bytes_accessed=10**7, transcendentals=2 * 10**6),
    )(queries, key_vectors, values, features, norm_gain, out_weight)


def solution(mesh):
    return jax.shard_map(
        attention,
        mesh=mesh,
        in_specs=(
            P("ctx", "head"),
            P("ctx", "head"),
            P("ctx", "head"),
            P("head", None, None),
            P("head"),
            P("head", None),
        ),
        out_specs=P(("ctx", "head"), None),
        check_vma=False,
    )
```

```python
import jax
import jax.numpy as jnp
from jax import lax
from jax.experimental import pallas as pl
from jax.experimental.pallas import tpu as pltpu
from jax.sharding import PartitionSpec as P

MESH = pl.DeviceIdType.MESH
F32 = jnp.float32
BF16 = jnp.bfloat16
BLK = 256
NX, NY, NZ = 4, 4, 8
NXY = NX * NY
SIZES = (2, 2, 2, 2)
CHUNKS = len(SIZES)
STARTS = tuple(sum(SIZES[:c]) for c in range(CHUNKS))
SCHEDULE = (
    ("line", 0, 2),
    ("line", 1, 1),
    ("prefix", 0, 0),
    ("line", 2, 0),
    ("prefix", 1, 1),
    ("line", 3, 0),
    ("prefix", 2, 0),
    ("prefix", 3, 0),
)
OUT_TILES = 1
EPSILON = 1e-05
ORDER = (4, 3, 5, 2, 6, 1, 7)


def dot(a, b, contract=((1,), (0,))):
    return lax.dot_general(a, b, (contract, ((), ())), preferred_element_type=F32)


def halves(squared):
    high = squared.astype(BF16)
    return high, (squared - high.astype(F32)).astype(BF16)


def kernel(
    q_hbm, k_hbm, v_hbm, f_hbm, gain_hbm, w_hbm, out_ref,
    q_ref, k_ref, v_ref, f_ref, gain_ref, w_ref, kft, qf, local, first,
    state_send, state_recv, line_send, line_recv, prefix_send, prefix_recv, att, gains, acc,
    load_sem, kv_sems, w_sems, s_ssem, s_rsem, l_ssem, l_rsem, p_ssem, p_rsem, a_ssem, a_rsem,
):
    heads, dh, m = f_ref.shape
    rows = q_ref.shape[0]
    width = heads * dh
    piece = m // NZ
    scale = dh ** (-0.25)
    log2e = 1.4426950408889634
    shift = 0.5 * (m.bit_length() - 1)
    me = lax.axis_index("ctx")
    core = lax.axis_index("head")
    peer = 1 - core
    z = lax.rem(me, NZ)
    w = me // NZ

    def at_z(d):
        return lax.rem(z + d, NZ)

    def z_device(d):
        return {"ctx": me - z + at_z(d)}

    def head_columns(h):
        return pl.ds(pl.multiple_of(h * dh, dh), dh)

    def heads_of(c):
        return pl.ds(STARTS[c], SIZES[c])

    own_rows = pl.ds(pl.multiple_of(core * width, width), width)

    def chunk_load(i, c):
        src, dst = ((k_hbm, k_ref), (v_hbm, v_ref))[i]
        cols = pl.ds(STARTS[c] * dh, SIZES[c] * dh)
        return pltpu.make_async_copy(src.at[:, cols], dst.at[:, cols], kv_sems.at[i, c])

    loads = [
        pltpu.make_async_copy(src, dst, load_sem.at[i])
        for i, (src, dst) in enumerate(
            ((f_hbm, f_ref), (q_hbm, q_ref), (gain_hbm, gain_ref), (w_hbm, w_ref.at[own_rows, :]))
        )
    ]
    loads[0].start()
    chunk_load(0, 0).start()
    chunk_load(1, 0).start()

    barrier = pltpu.get_barrier_semaphore()
    for d in range(1, NZ):
        pl.semaphore_signal(barrier, inc=1, device_id=z_device(d), device_id_type=MESH)

    def greet(t, carry):
        pl.semaphore_signal(barrier, inc=1, device_id={"ctx": t * NZ + z}, device_id_type=MESH)
        return carry

    lax.fori_loop(0, w, greet, 0)
    pl.semaphore_signal(barrier, inc=1, device_id={"head": peer}, device_id_type=MESH)

    w_copy = pltpu.make_async_remote_copy(
        src_ref=w_hbm, dst_ref=w_ref.at[own_rows, :], send_sem=w_sems.at[0], recv_sem=w_sems.at[1],
        device_id={"head": peer}, device_id_type=MESH,
    )

    def state_copy(c, d):
        return pltpu.make_async_remote_copy(
            src_ref=state_send.at[at_z(d), heads_of(c)], dst_ref=state_recv.at[z, heads_of(c)],
            send_sem=s_ssem.at[c], recv_sem=s_rsem.at[c],
            device_id=z_device(d), device_id_type=MESH,
        )

    def line_copy(c, t):
        return pltpu.make_async_remote_copy(
            src_ref=line_send.at[heads_of(c)], dst_ref=line_recv.at[w, heads_of(c)],
            send_sem=l_ssem.at[c, t], recv_sem=l_rsem.at[c, w],
            device_id={"ctx": t * NZ + z}, device_id_type=MESH,
        )

    def prefix_copy(c, d):
        return pltpu.make_async_remote_copy(
            src_ref=prefix_send.at[at_z(d), heads_of(c)], dst_ref=prefix_recv.at[z, heads_of(c)],
            send_sem=p_ssem.at[c], recv_sem=p_rsem.at[c],
            device_id=z_device(d), device_id_type=MESH,
        )

    def att_columns(owner, c):
        return pl.ds(pl.multiple_of(owner * width + STARTS[c] * dh, dh), SIZES[c] * dh)

    def att_copy(c):
        cols = att_columns(core, c)
        return pltpu.make_async_remote_copy(
            src_ref=att.at[peer, :, cols], dst_ref=att.at[peer, :, cols],
            send_sem=a_ssem.at[c], recv_sem=a_rsem.at[c],
            device_id={"head": peer}, device_id_type=MESH,
        )

    def arrival(ref, sem, device_id):
        return pltpu.make_async_remote_copy(
            src_ref=ref, dst_ref=ref, send_sem=sem, recv_sem=sem, device_id=device_id, device_id_type=MESH
        )

    def all_pieces(c, send_sem, recv_sem):
        ref = prefix_recv.at[pl.ds(0, NZ - 1), heads_of(c)]
        return pltpu.make_async_remote_copy(
            src_ref=ref, dst_ref=ref, send_sem=send_sem.at[c], recv_sem=recv_sem.at[c],
            device_id=z_device(1), device_id_type=MESH,
        )

    loads[0].wait()
    ones_row = jnp.ones((8, dh), BF16)

    def key_head(h):
        cols = head_columns(h)
        k = k_ref[:, cols]
        v = v_ref[:, cols]
        linear = dot(f_ref[h].T, k, ((1,), (1,)))
        wide = k.astype(F32)
        high, low = halves(wide * wide)
        squares = dot(jnp.ones((8, 2 * dh), BF16), jnp.concatenate([high, low], axis=1), ((1,), (1,)))[0:1]
        feats = jnp.exp2(
            linear * (scale * log2e) - (squares * (0.5 * scale * scale * log2e) + shift)
        ).astype(BF16)
        kft[h] = feats
        one = dot(feats[:, :BLK], v[:BLK])
        two = dot(feats[:, BLK:], v[BLK:])
        first[h] = one.astype(BF16)
        state_send[:, h] = (one + two).astype(BF16).reshape(NZ, piece, dh)

    for c in range(CHUNKS):
        chunk_load(0, c).wait()
        chunk_load(1, c).wait()
        if c == 0:
            for later in range(1, CHUNKS):
                chunk_load(0, later).start()
                chunk_load(1, later).start()
        for i in range(SIZES[c]):
            key_head(STARTS[c] + i)
        if c == 0:
            pl.semaphore_wait(barrier, NZ - 1 + NXY - 1 - w + 1)
        for d in ORDER:
            state_copy(c, d).start()
        state_recv[z, heads_of(c)] = state_send[z, heads_of(c)]
        if c == 0:
            for load in loads[1:]:
                load.start()
            w_copy.start()

    loads[1].wait()
    ones_square = jnp.ones((dh, dh), BF16)
    mask = lax.broadcasted_iota(jnp.int32, (BLK, BLK), 0) >= lax.broadcasted_iota(jnp.int32, (BLK, BLK), 1)

    def query_head(h, carry):
        cols = head_columns(h)
        q = q_ref[:, cols]
        wide = q.astype(F32)
        high, low = halves(wide * wide)
        squares = dot(high, ones_square) + dot(low, ones_square)
        away = squares * (0.5 * scale * scale * log2e) + shift
        linear = dot(q, f_ref[h])
        feats = jnp.exp2(
            linear * (scale * log2e) - jnp.concatenate([away] * (m // dh), axis=1)
        ).astype(BF16)
        qf[h] = feats
        for b in range(rows // BLK):
            span = slice(b * BLK, (b + 1) * BLK)
            scores = dot(feats[span], kft[h, :, span])
            weights = jnp.where(mask, scores, 0.0).astype(BF16)
            term = dot(weights, v_ref[span, cols])
            if b > 0:
                term = term + dot(feats[span], first[h])
            local[span, cols] = term
        return carry

    def query_chunk(c):
        lax.fori_loop(STARTS[c], STARTS[c] + SIZES[c], query_head, 0)

    def line_sum(c):
        all_pieces(c, s_ssem, s_rsem).wait_recv()
        total = jnp.zeros((SIZES[c], piece, dh), F32)
        for s in range(NZ):
            total = total + state_recv[s, heads_of(c)].astype(F32)
        line_send[heads_of(c)] = total.astype(BF16)

        def send(t, carry):
            line_copy(c, t).start()
            return carry

        lax.fori_loop(w + 1, NXY, send, 0)

    def prefixes(c):
        def one(s, running):
            arrival(line_recv.at[s, heads_of(c)], l_rsem.at[c, s], {"ctx": s * NZ + z}).wait_recv()
            return running + line_recv[s, heads_of(c)].astype(F32)

        running = lax.fori_loop(0, w, one, jnp.zeros((SIZES[c], piece, dh), F32))
        for s in range(NZ):
            prefix_send[s, heads_of(c)] = running.astype(BF16)
            running = running + state_recv[s, heads_of(c)].astype(F32)
        for d in ORDER:
            prefix_copy(c, d).start()
        prefix_recv[z, heads_of(c)] = prefix_send[z, heads_of(c)]

    def last_chunk(c):
        all_pieces(c, p_ssem, p_rsem).wait_recv()
        for b in (peer, core):
            span = pl.ds(pl.multiple_of(b * BLK, BLK), BLK)
            for i in range(SIZES[c]):
                h = STARTS[c] + i
                numerator = local[span, head_columns(h)] + dot(qf[h, span], prefix_recv[:, h].reshape(m, dh))
                mean = jnp.mean(numerator * numerator, axis=-1, keepdims=True)
                att[b, :, pl.ds(pl.multiple_of(core * width + h * dh, dh), dh)] = (
                    numerator * lax.rsqrt(mean + EPSILON) * gains[h : h + 1, :]
                ).astype(BF16)
            if b is peer:
                att_copy(c).start()

    def att_wait(c):
        cols = att_columns(peer, c)
        arrival(att.at[core, :, cols], a_rsem.at[c], {"head": peer}).wait_recv()

    tile = w_ref.shape[1] // OUT_TILES

    def project(blocks, start, end):
        def one(n, carry):
            cols = pl.ds(pl.multiple_of(n * tile, tile), tile)
            total = None if start else acc[:, cols]
            for block in blocks:
                product = dot(att[core, :, block], w_ref[block, cols])
                total = product if total is None else total + product
            if end:
                out_ref[:, cols] = total.astype(BF16)
            else:
                acc[:, cols] = total
            return carry

        lax.fori_loop(0, OUT_TILES, one, 0, unroll=True)

    waiting = list(range(CHUNKS))
    for name, c, queries in SCHEDULE:
        for _ in range(queries):
            query_chunk(waiting.pop(0))
        if name == "line":
            line_sum(c)
        else:
            prefixes(c)
    loads[2].wait()
    wide_gain = gain_ref[...].astype(F32)
    for h in range(heads):
        gains[h : h + 1, :] = wide_gain[h * dh : (h + 1) * dh].reshape(1, dh)
    loads[3].wait()
    w_copy.wait()

    for c in range(CHUNKS):
        all_pieces(c, s_ssem, s_rsem).wait_send()

        def sent(t, carry):
            line_copy(c, t).wait_send()
            return carry

        lax.fori_loop(w + 1, NXY, sent, 0)

    for c in range(CHUNKS):
        last_chunk(c)
        if c > 0:
            att_copy(c - 1).wait_send()
        if c == 0:
            project([att_columns(core, c)], True, False)
        else:
            att_wait(c - 1)
            project([att_columns(core, c), att_columns(peer, c - 1)], False, False)
    for c in range(CHUNKS):
        all_pieces(c, p_ssem, p_rsem).wait_send()
    att_wait(CHUNKS - 1)
    project([att_columns(peer, CHUNKS - 1)], False, True)

    att_copy(CHUNKS - 1).wait_send()


def attention(queries, key_vectors, values, features, norm_gain, out_weight):
    heads, dh, m = features.shape
    rows, width = queries.shape
    full, columns = 2 * width, out_weight.shape[1]
    slab = (heads, m // NZ, dh)
    dma = pltpu.SemaphoreType.DMA
    return pl.pallas_call(
        kernel,
        out_shape=pltpu.VMEM((rows // 2, columns), BF16),
        in_specs=[pl.BlockSpec(memory_space=pl.ANY)] * 6,
        out_specs=pl.BlockSpec(memory_space=pltpu.VMEM),
        scratch_shapes=[
            pltpu.VMEM((rows, width), BF16),
            pltpu.VMEM((rows, width), BF16),
            pltpu.VMEM((rows, width), BF16),
            pltpu.VMEM((heads, dh, m), BF16),
            pltpu.VMEM((width,), BF16),
            pltpu.VMEM((full, columns), BF16),
            pltpu.VMEM((heads, m, rows), BF16),
            pltpu.VMEM((heads, rows, m), BF16),
            pltpu.VMEM((rows, width), F32),
            pltpu.VMEM((heads, m, dh), BF16),
            pltpu.VMEM((NZ,) + slab, BF16),
            pltpu.VMEM((NZ,) + slab, BF16),
            pltpu.VMEM(slab, BF16),
            pltpu.VMEM((NXY,) + slab, BF16),
            pltpu.VMEM((NZ,) + slab, BF16),
            pltpu.VMEM((NZ,) + slab, BF16),
            pltpu.VMEM((2, rows // 2, full), BF16),
            pltpu.VMEM((heads, dh), F32),
            pltpu.VMEM((rows // 2, columns), F32),
            dma((4,)),
            dma((2, CHUNKS)),
            dma((2,)),
            dma((CHUNKS,)),
            dma((CHUNKS,)),
            dma((CHUNKS, NXY)),
            dma((CHUNKS, NXY)),
            dma((CHUNKS,)),
            dma((CHUNKS,)),
            dma((CHUNKS,)),
            dma((CHUNKS,)),
        ],
        compiler_params=pltpu.CompilerParams(
            collective_id=0, has_side_effects=True, vmem_limit_bytes=60 * 1024 * 1024
        ),
        cost_estimate=pl.CostEstimate(flops=4 * 10**9, bytes_accessed=10**7, transcendentals=2 * 10**6),
    )(queries, key_vectors, values, features, norm_gain, out_weight)


def solution(mesh):
    return jax.shard_map(
        attention,
        mesh=mesh,
        in_specs=(
            P("ctx", "head"),
            P("ctx", "head"),
            P("ctx", "head"),
            P("head", None, None),
            P("head"),
            P("head", None),
        ),
        out_specs=P(("ctx", "head"), None),
        check_vma=False,
    )
```
